256 devices in a mesh: row: 16 (over z_hi, y, core), col: 4 (over z_lo), depth: 4 (over x).
Axes of the slice: x: 4, y: 4, z: 8 (z_hi: 2, z_lo: 4; z = z_hi * 4 + z_lo), core: 2. Of those that a mesh axis runs over, the one named last changes fastest.
Arguments:
- packed: bfloat16 [1024, 128, 128], P(('row', 'col', 'depth')), may hold values from -6 to 6
- block_index: int32 [8, 256], replicated, may hold values from 0 to 1023, as said below
- block_sign: int32 [8, 256], replicated, may hold values from -1 to 1, as said below
- ovov: bfloat16 [32768, 32768], P('row', ('col', 'depth')), may hold values from -0.03125 to 0.03125
- residual_in: bfloat16 [1024, 32768], P('row', ('col', 'depth')), may hold values from -6 to 6
Outputs:
- updated: bfloat16 [1024, 32768], P('row', ('col', 'depth'))
The draws below stay inside these ranges and needn't reach their ends.
Inputs may be any that keep to these rules, and one draw needn't show every extreme that they name: `block_index`: each packed block is named by exactly two entries. Entries in block column s name packed blocks from (s // 16) * 8 * 8 to (s // 16 + 1) * 8 * 8 - 1. `block_sign`: every entry is 1 or -1; the two entries that name one packed block have opposite signs.
All inputs are finite; a program needn't handle non-finite values.
Results may differ from the reference program's by a relative error of at most 0.001.
Values may be sent and summed in bfloat16 or wider, within the bound.
A program may use at most 64 MiB of HBM per device.

```python
import jax
import jax.numpy as jnp

BS = 128
ROWS = 1024
OV = 32768
RB = 8
KB = 256
KBQ = 16
NPACK = 1024


def pair_tables(key):
    groups = KB // KBQ
    per_group = RB * KBQ
    keys = jax.random.split(key, groups)
    order = jax.vmap(lambda k: jax.random.permutation(k, per_group))(keys).astype(jnp.int32)
    flips = jax.random.randint(jax.random.fold_in(key, 11), (groups, per_group // 2), 0, 2).astype(jnp.int32)
    base = (jnp.arange(groups, dtype=jnp.int32) * (per_group // 2))[:, None]
    partner = order // 2
    index = base + partner
    first = jnp.take_along_axis(flips, partner, axis=1)
    sign = (1 - 2 * first) * (1 - 2 * (order % 2))
    index = index.reshape(groups, RB, KBQ).transpose(1, 0, 2).reshape(RB, KB)
    sign = sign.reshape(groups, RB, KBQ).transpose(1, 0, 2).reshape(RB, KB)
    return (index.astype(jnp.int32), sign.astype(jnp.int32))


def draw_block_index(key, part):
    return pair_tables(key)[0]


def draw_block_sign(key, part):
    return pair_tables(key)[1]


def levels(key, shape, pieces, least, top_value):
    factor_of = 1.0
    for position, shards_of in pieces:
        steps = jax.random.uniform(jax.random.fold_in(jax.random.fold_in(key, 6), position), (shards_of,), jnp.float32, least / len(pieces), top_value / len(pieces))
        factor_of = factor_of * jnp.repeat(jnp.exp(steps), shape[position] // shards_of).reshape((-1,) + (1,) * (len(shape) - 1 - position))
    return factor_of


def gaussian(own_key, dims, scale, reach, pieces=(), kind=jnp.bfloat16):
    values = scale * jax.random.normal(own_key, dims, jnp.float32)
    if pieces:
        values = values * levels(own_key, dims, pieces, -0.22, 0.18)
    return jnp.clip(values, -reach, reach).astype(kind)


def setup_inputs(seed: int = 0) -> dict:
    arg_keys = jax.random.split(jax.random.key(seed), 6)
    packed = gaussian(arg_keys[0], (NPACK, BS, BS), 1.0, 6.0, ((0, 256),))
    block_index = draw_block_index(jax.random.fold_in(arg_keys[5], 71), 0)
    block_sign = draw_block_sign(jax.random.fold_in(arg_keys[5], 71), 0)
    ovov = gaussian(arg_keys[3], (OV, OV), OV ** -0.5, 0.03125, ((0, 16), (1, 16)))
    residual_in = gaussian(arg_keys[4], (ROWS, OV), 1.0, 6.0, ((0, 16), (1, 16)))
    return {"packed": packed, "block_index": block_index, "block_sign": block_sign, "ovov": ovov, "residual_in": residual_in}


def reference(packed, block_index, block_sign, ovov, residual_in):
    blocks = packed[block_index.reshape(-1)].astype(jnp.float32)
    blocks = blocks * block_sign.reshape(-1).astype(jnp.float32)[:, None, None]
    slab = blocks.reshape(RB, KB, BS, BS).transpose(0, 2, 1, 3).reshape(ROWS, OV).astype(jnp.bfloat16)
    product = jnp.dot(slab, ovov, preferred_element_type=jnp.float32)
    return (residual_in.astype(jnp.float32) + product).astype(jnp.bfloat16)
```

```python
import math

import jax
import jax.numpy as jnp
from jax import lax
from jax.experimental import pallas as pl
from jax.experimental.pallas import tpu as pltpu
from jax.sharding import PartitionSpec as P

MESH = pl.DeviceIdType.MESH
F32 = jnp.float32
BF16 = jnp.bfloat16
I16 = jnp.int16
I32 = jnp.int32

NY, NX, NZ = 4, 4, 4
BLOCK = 128
HALVES = 8
XF = 6
PANELS = 2
PW = 1024
MW = 512
SHARE = 64
TILES = MW // 128
MROWS = SHARE * TILES + 16
STEPS = 64.0
TOP = 32000.0
LN2 = math.log(2.0)


def encode(tiles):
    split = [t.reshape(SHARE // 16, 16, 128) for t in tiles]
    top = jnp.max(jnp.abs(split[0]), axis=0)
    for t in split[1:]:
        top = jnp.maximum(top, jnp.max(jnp.abs(t), axis=0))
    code = jnp.ceil(jnp.log(jnp.maximum(top, 1e-30)) * (STEPS / LN2)) + 1.0
    inverse = jnp.exp(code * (-LN2 / STEPS)) * TOP
    values = [
        jnp.round(t * inverse[None]).astype(I32).astype(I16).reshape(SHARE, 128) for t in split
    ]
    return values, code.astype(I32).astype(I16)


def decode(ref):
    code = ref[pl.ds(SHARE * TILES, 16), :].astype(I32).astype(F32)
    scale = jnp.exp(code * (LN2 / STEPS)) * (1.0 / TOP)
    out = []
    for t in range(TILES):
        v = ref[pl.ds(t * SHARE, SHARE), :].astype(I32).astype(F32)
        out.append((v.reshape(SHARE // 16, 16, 128) * scale[None]).reshape(SHARE, 128))
    return out


def add(a, b):
    return [x + y for x, y in zip(a, b)]


def kernel(
    index_ref, sign_ref, packed_ref, ovov_ref, residual_ref, out_ref,
    gath, ovov, resid, slab, acc, d2d, msend, mrecv,
    local_sem, gs, gr, ds, dr, ms, mr,
):
    row = lax.axis_index("row")
    col = lax.axis_index("col")
    dep = lax.axis_index("depth")
    core = lax.rem(row, 2)
    y = lax.rem(row // 2, NY)
    zh = row // (2 * NY)

    def row_of(zh_, y_, core_):
        return (zh_ * NY + y_) * 2 + core_

    sibling = {"row": row_of(zh, y, 1 - core)}
    y_up = {"row": row_of(zh, lax.rem(y + 1, NY), core)}
    y_down = {"row": row_of(zh, lax.rem(y + NY - 1, NY), core)}
    z_far = {"row": row_of(1 - zh, y, core)}
    dep_up, dep_down = lax.rem(dep + 1, NX), lax.rem(dep + NX - 1, NX)
    dep_far = lax.rem(dep + 2, NX)
    x_up, x_down = {"depth": dep_up}, {"depth": dep_down}
    z_up = {"row": row_of(lax.rem(zh + (col + 1) // NZ, 2), y, core), "col": lax.rem(col + 1, NZ)}
    z_down = {
        "row": row_of(lax.rem(zh + 1 + (col + NZ - 1) // NZ, 2), y, core),
        "col": lax.rem(col + NZ - 1, NZ),
    }

    def slot(c, d):
        return (c * NX + d) * HALVES

    mine = slot(col, dep)
    own_copy = pltpu.make_async_copy(packed_ref, gath.at[pl.ds(mine, HALVES)], local_sem.at[0])
    own_copy.start()
    res_copy = pltpu.make_async_copy(residual_ref, resid, local_sem.at[1])
    ovov_copy = pltpu.make_async_copy(ovov_ref, ovov, local_sem.at[2])
    ovov_copy.start()
    res_copy.start()

    barrier = pltpu.get_barrier_semaphore()
    peers = (sibling, y_up, y_down, z_far, x_up, x_down, z_up, z_down)
    for p in peers:
        pl.semaphore_signal(barrier, inc=1, device_id=p, device_id_type=MESH)
    pl.semaphore_wait(barrier, len(peers))
    own_copy.wait()

    sends = []

    def guarded(cond, fn):
        if cond is None:
            fn()
        else:
            pl.when(cond)(fn)

    def send(cond, first, count, sem, target):
        part = gath.at[pl.ds(first, count)]
        number = len(sends)
        copy = pltpu.make_async_remote_copy(
            part, part, gs.at[number], gr.at[sem], device_id=target, device_id_type=MESH
        )
        sends.append((cond, copy))
        guarded(cond, copy.start)

    def arrive(cond, first, count, sem):
        part = gath.at[pl.ds(first, count)]
        copy = pltpu.make_async_remote_copy(
            part, part, gs.at[0], gr.at[sem], device_id=sibling, device_id_type=MESH
        )
        guarded(cond, copy.wait_recv)

    def sem_of(j, kind):
        return j * 8 + kind

    def both(a, b):
        return b if a is None else jnp.logical_and(a, b)

    can_up, can_down = col < NZ - 1, col > 0

    def rows_at(k):
        if k == 0:
            return [(None, col, 0)]
        return [(col >= k, col - k, 1), (col + k < NZ, col + k, -1)]

    def pass_on(cond, way, first, count, sem):
        if way >= 0:
            send(both(cond, can_up), first, count, sem, z_up)
        if way <= 0:
            send(both(cond, can_down), first, count, sem, z_down)

    def x_count(k):
        return HALVES if k == 0 else XF

    def step_share(k):
        for cond, j, way in rows_at(k):
            if k > 0:
                arrive(cond, slot(j, dep), HALVES, sem_of(j, 0))
            send(cond, slot(j, dep), x_count(k), sem_of(j, 1), x_up)
            send(cond, slot(j, dep), x_count(k), sem_of(j, 2), x_down)
            pass_on(cond, way, slot(j, dep), HALVES, sem_of(j, 0))

    def step_near(k):
        n = x_count(k)
        for cond, j, way in rows_at(k):
            arrive(cond, slot(j, dep_down), n, sem_of(j, 1))
            send(cond, slot(j, dep_down), n // 2, sem_of(j, 3), x_up)
            arrive(cond, slot(j, dep_up), n, sem_of(j, 2))
            send(cond, slot(j, dep_up) + n // 2, n // 2, sem_of(j, 4), x_down)

    rest = HALVES - XF

    def step_rest_near(k):
        for cond, j, way in rows_at(k):
            for kind, d in ((5, dep_down), (6, dep_up)):
                if k > 0:
                    arrive(cond, slot(j, d) + XF, rest, sem_of(j, kind))
                pass_on(cond, way, slot(j, d) + XF, rest, sem_of(j, kind))

    def step_far(k):
        n = x_count(k)
        for cond, j, way in rows_at(k):
            arrive(cond, slot(j, dep_far), n // 2, sem_of(j, 3))
            arrive(cond, slot(j, dep_far) + n // 2, n // 2, sem_of(j, 4))
            if k > 0:
                arrive(cond, slot(j, dep_far) + XF, rest, sem_of(j, 7))
            pass_on(cond, way, slot(j, dep_far) + XF, rest, sem_of(j, 7))

    step_share(0)
    step_share(1)
    step_near(0)
    step_rest_near(0)
    step_share(2)
    step_near(1)
    step_far(0)
    step_rest_near(1)
    step_share(3)
    step_near(2)
    step_far(1)
    step_rest_near(2)
    step_near(3)
    step_far(2)
    step_rest_near(3)
    step_far(3)
    for cond, copy in sends:
        guarded(cond, copy.wait_send)
    ovov_copy.wait()

    def block_row(h, i):
        yy = lax.rem(y + (2, 1, NY - 1, 0)[i], NY)
        return ((1 - zh) if h == 0 else zh) * NY + yy

    blocks_per_row = ovov.shape[0] // BLOCK

    def build(h):
        for i in range(4):
            r = block_row(h, i)

            @pl.loop(0, blocks_per_row)
            def _(s):
                at = row * blocks_per_row + s
                p = lax.rem(index_ref[r, at], gath.shape[0] // 2)
                tile = gath[pl.ds(2 * p, 2)].reshape(BLOCK, BLOCK)
                sign = sign_ref[r, at].astype(F32)
                slab[pl.ds(i * BLOCK, BLOCK), pl.ds(pl.multiple_of(s * BLOCK, BLOCK), BLOCK)] = (
                    tile.astype(F32) * sign
                ).astype(BF16)

    my_rows = pl.ds(pl.multiple_of(core * SHARE, SHARE), SHARE)
    their_rows = pl.ds(pl.multiple_of((1 - core) * SHARE, SHARE), SHARE)
    units = [(h, q) for h in range(2) for q in range(PANELS)]
    NT = 256
    core_copies = []

    def multiply(u, part):
        h, q = units[u]

        @pl.loop(0, PW // NT)
        def _(n):
            here = pl.ds(pl.multiple_of(n * NT, NT), NT)
            there = pl.ds(pl.multiple_of(q * PW + n * NT, NT), NT)
            t = jnp.dot(
                slab[pl.ds(part * 256, 256), :], ovov[:, there], preferred_element_type=F32
            )
            for i in range(2):
                acc[u, part * 2 + i, :, here] = t[i * BLOCK : (i + 1) * BLOCK]

        copy = pltpu.make_async_remote_copy(
            acc.at[u, pl.ds(part * 2, 2), their_rows],
            d2d.at[u, pl.ds(part * 2, 2)],
            ds.at[u * 2 + part],
            dr.at[u * 2 + part],
            device_id=sibling,
            device_id_type=MESH,
        )
        copy.start()
        core_copies.append(copy)

    def summed(u, i, half):
        return [
            acc[u, i, my_rows, pl.ds(half * MW + t * 128, 128)]
            + d2d[u, i, :, pl.ds(half * MW + t * 128, 128)]
            for t in range(TILES)
        ]

    messages = {}

    def message_copy(number, target):
        return pltpu.make_async_remote_copy(
            msend.at[number], mrecv.at[number], ms.at[number], mr.at[number],
            device_id=target, device_id_type=MESH,
        )

    def post(number, tiles, target):
        values, code = encode(tiles)
        for t in range(TILES):
            msend[number, pl.ds(t * SHARE, SHARE), :] = values[t]
        msend[number, pl.ds(TILES * SHARE, 16), :] = code
        copy = message_copy(number, target)
        copy.start()
        messages[number] = copy

    def fetch(number):
        message_copy(number, sibling).wait_recv()
        return decode(mrecv.at[number])

    A, B = 0, 1
    def first_sends(u):
        core_copies[2 * u].wait_recv()
        post(u * 6 + 0, summed(u, 0, A), y_up)
        post(u * 6 + 1, summed(u, 0, B), y_down)
        post(u * 6 + 2, summed(u, 1, B), y_up)
        core_copies[2 * u + 1].wait_recv()
        post(u * 6 + 3, summed(u, 2, A), y_down)

    def second_sends(u):
        post(u * 6 + 4, add(summed(u, 1, A), fetch(u * 6 + 0)), y_up)
        post(u * 6 + 5, add(summed(u, 2, B), fetch(u * 6 + 1)), y_down)

    zbase = len(units) * 6

    def finish(u):
        h, q = units[u]
        total_a = add(add(summed(u, 3, A), fetch(u * 6 + 3)), fetch(u * 6 + 4))
        if h == 0:
            post(zbase + q * 2, total_a, z_far)
        else:
            store(q, A, add(total_a, fetch(zbase + q * 2)))
        total_b = add(add(summed(u, 3, B), fetch(u * 6 + 2)), fetch(u * 6 + 5))
        if h == 0:
            post(zbase + q * 2 + 1, total_b, z_far)
        else:
            store(q, B, add(total_b, fetch(zbase + q * 2 + 1)))

    def store(q, half, tiles):
        for t in range(TILES):
            at = pl.ds(q * PW + half * MW + t * 128, 128)
            out_ref[:, at] = (resid[:, at].astype(F32) + tiles[t]).astype(BF16)

    build(0)
    multiply(0, 0)
    multiply(0, 1)
    first_sends(0)
    multiply(1, 0)
    multiply(1, 1)
    second_sends(0)
    first_sends(1)
    build(1)
    multiply(2, 0)
    multiply(2, 1)
    finish(0)
    second_sends(1)
    first_sends(2)
    multiply(3, 0)
    multiply(3, 1)
    finish(1)
    second_sends(2)
    first_sends(3)
    second_sends(3)
    res_copy.wait()
    finish(2)
    finish(3)

    for copy in core_copies:
        copy.wait_send()
    for number in sorted(messages):
        messages[number].wait_send()


def per_device(packed, block_index, block_sign, ovov, residual_in):
    share, depth, width = packed.shape[0], ovov.shape[0], ovov.shape[1]
    plane = NZ * NX
    count = 4 * 6 + 4
    n_sends = 64
    anywhere = pl.BlockSpec(memory_space=pl.ANY)
    scalars = pl.BlockSpec(memory_space=pltpu.SMEM)
    return pl.pallas_call(
        kernel,
        out_shape=jax.ShapeDtypeStruct(residual_in.shape, BF16),
        in_specs=[scalars, scalars, anywhere, anywhere, anywhere],
        out_specs=pl.BlockSpec(memory_space=pltpu.VMEM),
        scratch_shapes=[
            pltpu.VMEM((plane * HALVES, BLOCK // 2, BLOCK), BF16),
            pltpu.VMEM((depth, width), BF16),
            pltpu.VMEM(residual_in.shape, BF16),
            pltpu.VMEM((4 * BLOCK, depth), BF16),
            pltpu.VMEM((4, 4, BLOCK, PW), F32),
            pltpu.VMEM((4, 4, SHARE, PW), F32),
            pltpu.VMEM((count, MROWS, 128), I16),
            pltpu.VMEM((count, MROWS, 128), I16),
            pltpu.SemaphoreType.DMA((3,)),
            pltpu.SemaphoreType.DMA((n_sends,)),
            pltpu.SemaphoreType.DMA((NZ * 8,)),
            pltpu.SemaphoreType.DMA((8,)),
            pltpu.SemaphoreType.DMA((8,)),
            pltpu.SemaphoreType.DMA((count,)),
            pltpu.SemaphoreType.DMA((count,)),
        ],
        compiler_params=pltpu.CompilerParams(
            collective_id=0, has_side_effects=True, vmem_limit_bytes=52 << 20
        ),
        cost_estimate=pl.CostEstimate(
            flops=2 * 1024 * depth * width, bytes_accessed=depth * width * 2, transcendentals=0
        ),
    )(
        block_index,
        block_sign,
        packed.reshape(share * 2, BLOCK // 2, BLOCK),
        ovov,
        residual_in,
    )


def solution(mesh):
    in_specs = (
        P(("row", "col", "depth"), None, None),
        P(),
        P(),
        P("row", ("col", "depth")),
        P("row", ("col", "depth")),
    )
    out_specs = P("row", ("col", "depth"))
    return jax.shard_map(
        per_device, mesh=mesh, in_specs=in_specs, out_specs=out_specs, check_vma=False
    )
```

```python
import math

import jax
import jax.numpy as jnp
from jax import lax
from jax.experimental import pallas as pl
from jax.experimental.pallas import tpu as pltpu
from jax.sharding import PartitionSpec as P

MESH = pl.DeviceIdType.MESH
F32 = jnp.float32
BF16 = jnp.bfloat16
I16 = jnp.int16
I32 = jnp.int32

NY, NX, NZ = 4, 4, 4
BLOCK = 128
HALVES = 8
XF = 6
PANELS = 2
PW = 1024
MW = 512
SHARE = 64
TILES = MW // 128
MROWS = SHARE * TILES + 16
STEPS = 64.0
TOP = 32000.0
LN2 = math.log(2.0)


def encode(tiles):
    split = [t.reshape(SHARE // 16, 16, 128) for t in tiles]
    top = jnp.max(jnp.abs(split[0]), axis=0)
    for t in split[1:]:
        top = jnp.maximum(top, jnp.max(jnp.abs(t), axis=0))
    code = jnp.ceil(jnp.log(jnp.maximum(top, 1e-30)) * (STEPS / LN2)) + 1.0
    inverse = jnp.exp(code * (-LN2 / STEPS)) * TOP
    values = [
        jnp.round(t * inverse[None]).astype(I32).astype(I16).reshape(SHARE, 128) for t in split
    ]
    return values, code.astype(I32).astype(I16)


def decode(ref):
    code = ref[pl.ds(SHARE * TILES, 16), :].astype(I32).astype(F32)
    scale = jnp.exp(code * (LN2 / STEPS)) * (1.0 / TOP)
    out = []
    for t in range(TILES):
        v = ref[pl.ds(t * SHARE, SHARE), :].astype(I32).astype(F32)
        out.append((v.reshape(SHARE // 16, 16, 128) * scale[None]).reshape(SHARE, 128))
    return out


def add(a, b):
    return [x + y for x, y in zip(a, b)]


def kernel(
    index_hbm, sign_hbm, packed_ref, ovov_ref, residual_ref, out_ref,
    index_ref, sign_ref, gath, ovov, resid, slab, acc, d2d, msend, mrecv,
    local_sem, gs, gr, ds, dr, ms, mr,
):
    row = lax.axis_index("row")
    col = lax.axis_index("col")
    dep = lax.axis_index("depth")
    core = lax.rem(row, 2)
    y = lax.rem(row // 2, NY)
    zh = row // (2 * NY)

    def row_of(zh_, y_, core_):
        return (zh_ * NY + y_) * 2 + core_

    sibling = {"row": row_of(zh, y, 1 - core)}
    y_up = {"row": row_of(zh, lax.rem(y + 1, NY), core)}
    y_down = {"row": row_of(zh, lax.rem(y + NY - 1, NY), core)}
    z_far = {"row": row_of(1 - zh, y, core)}
    dep_up, dep_down = lax.rem(dep + 1, NX), lax.rem(dep + NX - 1, NX)
    dep_far = lax.rem(dep + 2, NX)
    x_up, x_down = {"depth": dep_up}, {"depth": dep_down}
    z_up = {"row": row_of(lax.rem(zh + (col + 1) // NZ, 2), y, core), "col": lax.rem(col + 1, NZ)}
    z_down = {
        "row": row_of(lax.rem(zh + 1 + (col + NZ - 1) // NZ, 2), y, core),
        "col": lax.rem(col + NZ - 1, NZ),
    }

    def slot(c, d):
        return (c * NX + d) * HALVES

    mine = slot(col, dep)
    own_copy = pltpu.make_async_copy(packed_ref, gath.at[pl.ds(mine, HALVES)], local_sem.at[0])
    own_copy.start()
    index_copy = pltpu.make_async_copy(index_hbm, index_ref, local_sem.at[3])
    sign_copy = pltpu.make_async_copy(sign_hbm, sign_ref, local_sem.at[4])
    index_copy.start()
    sign_copy.start()
    res_copy = pltpu.make_async_copy(residual_ref, resid, local_sem.at[1])
    ovov_copy = pltpu.make_async_copy(ovov_ref, ovov, local_sem.at[2])
    ovov_copy.start()
    res_copy.start()

    barrier = pltpu.get_barrier_semaphore()
    peers = (sibling, y_up, y_down, z_far, x_up, x_down, z_up, z_down)
    for p in peers:
        pl.semaphore_signal(barrier, inc=1, device_id=p, device_id_type=MESH)
    pl.semaphore_wait(barrier, len(peers))
    own_copy.wait()

    sends = []

    def guarded(cond, fn):
        if cond is None:
            fn()
        else:
            pl.when(cond)(fn)

    def send(cond, first, count, sem, target):
        part = gath.at[pl.ds(first, count)]
        number = len(sends)
        copy = pltpu.make_async_remote_copy(
            part, part, gs.at[number], gr.at[sem], device_id=target, device_id_type=MESH
        )
        sends.append((cond, copy))
        guarded(cond, copy.start)

    def arrive(cond, first, count, sem):
        part = gath.at[pl.ds(first, count)]
        copy = pltpu.make_async_remote_copy(
            part, part, gs.at[0], gr.at[sem], device_id=sibling, device_id_type=MESH
        )
        guarded(cond, copy.wait_recv)

    def sem_of(j, kind):
        return j * 8 + kind

    def both(a, b):
        return b if a is None else jnp.logical_and(a, b)

    can_up, can_down = col < NZ - 1, col > 0

    def rows_at(k):
        if k == 0:
            return [(None, col, 0)]
        return [(col >= k, col - k, 1), (col + k < NZ, col + k, -1)]

    def pass_on(cond, way, first, count, sem):
        if way >= 0:
            send(both(cond, can_up), first, count, sem, z_up)
        if way <= 0:
            send(both(cond, can_down), first, count, sem, z_down)

    def x_count(k):
        return HALVES if k == 0 else XF

    def step_share(k):
        for cond, j, way in rows_at(k):
            if k > 0:
                arrive(cond, slot(j, dep), HALVES, sem_of(j, 0))
            send(cond, slot(j, dep), x_count(k), sem_of(j, 1), x_up)
            send(cond, slot(j, dep), x_count(k), sem_of(j, 2), x_down)
            pass_on(cond, way, slot(j, dep), HALVES, sem_of(j, 0))

    def step_near(k):
        n = x_count(k)
        for cond, j, way in rows_at(k):
            arrive(cond, slot(j, dep_down), n, sem_of(j, 1))
            send(cond, slot(j, dep_down), n // 2, sem_of(j, 3), x_up)
            arrive(cond, slot(j, dep_up), n, sem_of(j, 2))
            send(cond, slot(j, dep_up) + n // 2, n // 2, sem_of(j, 4), x_down)

    rest = HALVES - XF

    def step_rest_near(k):
        for cond, j, way in rows_at(k):
            for kind, d in ((5, dep_down), (6, dep_up)):
                if k > 0:
                    arrive(cond, slot(j, d) + XF, rest, sem_of(j, kind))
                pass_on(cond, way, slot(j, d) + XF, rest, sem_of(j, kind))

    def step_far(k):
        n = x_count(k)
        for cond, j, way in rows_at(k):
            arrive(cond, slot(j, dep_far), n // 2, sem_of(j, 3))
            arrive(cond, slot(j, dep_far) + n // 2, n // 2, sem_of(j, 4))
            if k > 0:
                arrive(cond, slot(j, dep_far) + XF, rest, sem_of(j, 7))
            pass_on(cond, way, slot(j, dep_far) + XF, rest, sem_of(j, 7))

    step_share(0)
    step_share(1)
    step_near(0)
    step_rest_near(0)
    step_share(2)
    step_near(1)
    step_far(0)
    step_rest_near(1)
    step_share(3)
    step_near(2)
    step_far(1)
    step_rest_near(2)
    step_near(3)
    step_far(2)
    step_rest_near(3)
    step_far(3)
    for cond, copy in sends:
        guarded(cond, copy.wait_send)
    ovov_copy.wait()
    index_copy.wait()
    sign_copy.wait()

    def block_row(h, i):
        yy = lax.rem(y + (2, 1, NY - 1, 0)[i], NY)
        return ((1 - zh) if h == 0 else zh) * NY + yy

    blocks_per_row = ovov.shape[0] // BLOCK
    HALF = 4 * SHARE

    def build(h):
        for i in range(4):
            r = block_row(h, i)

            @pl.loop(0, blocks_per_row)
            def _(s):
                at = row * blocks_per_row + s
                p = lax.rem(index_ref[r, at], gath.shape[0] // 2)
                sign = sign_ref[r, at].astype(F32)
                there = pl.ds(pl.multiple_of(s * BLOCK, BLOCK), BLOCK)
                for part, c in ((0, 1 - core), (1, core)):
                    tile = gath[2 * p + c]
                    slab[pl.ds(part * HALF + i * SHARE, SHARE), there] = (
                        tile.astype(F32) * sign
                    ).astype(BF16)

    units = [(h, q) for h in range(2) for q in range(PANELS)]
    core_copies = []

    def multiply(u, part):
        h, q = units[u]
        acc[u, part] = jnp.dot(
            slab[pl.ds(part * HALF, HALF), :],
            ovov[:, pl.ds(q * PW, PW)],
            preferred_element_type=F32,
        )
        if part == 1:
            return
        for w in range(2):
            rows = pl.ds(w * 2 * SHARE, 2 * SHARE)
            copy = pltpu.make_async_remote_copy(
                acc.at[u, 0, rows],
                d2d.at[u, rows],
                ds.at[u * 2 + w],
                dr.at[u * 2 + w],
                device_id=sibling,
                device_id_type=MESH,
            )
            copy.start()
            core_copies.append(copy)

    def summed(u, i, half):
        rows = pl.ds(i * SHARE, SHARE)
        out = []
        for t in range(TILES):
            at = pl.ds(half * MW + t * 128, 128)
            out.append(acc[u, 1, rows, at] + d2d[u, rows, at])
        return out

    messages = {}

    def message_copy(number, target):
        return pltpu.make_async_remote_copy(
            msend.at[number], mrecv.at[number], ms.at[number], mr.at[number],
            device_id=target, device_id_type=MESH,
        )

    def post(number, tiles, target):
        values, code = encode(tiles)
        for t in range(TILES):
            msend[number, pl.ds(t * SHARE, SHARE), :] = values[t]
        msend[number, pl.ds(TILES * SHARE, 16), :] = code
        copy = message_copy(number, target)
        copy.start()
        messages[number] = copy

    def fetch(number):
        message_copy(number, sibling).wait_recv()
        return decode(mrecv.at[number])

    A, B = 0, 1
    def first_sends(u):
        core_copies[2 * u].wait_recv()
        post(u * 6 + 0, summed(u, 0, A), y_up)
        post(u * 6 + 1, summed(u, 0, B), y_down)
        post(u * 6 + 2, summed(u, 1, B), y_up)
        core_copies[2 * u + 1].wait_recv()
        post(u * 6 + 3, summed(u, 2, A), y_down)

    def second_sends(u):
        post(u * 6 + 4, add(summed(u, 1, A), fetch(u * 6 + 0)), y_up)
        post(u * 6 + 5, add(summed(u, 2, B), fetch(u * 6 + 1)), y_down)

    zbase = len(units) * 6

    def finish(u):
        h, q = units[u]
        total_a = add(add(summed(u, 3, A), fetch(u * 6 + 3)), fetch(u * 6 + 4))
        if h == 0:
            post(zbase + q * 2, total_a, z_far)
        else:
            store(q, A, add(total_a, fetch(zbase + q * 2)))
        total_b = add(add(summed(u, 3, B), fetch(u * 6 + 2)), fetch(u * 6 + 5))
        if h == 0:
            post(zbase + q * 2 + 1, total_b, z_far)
        else:
            store(q, B, add(total_b, fetch(zbase + q * 2 + 1)))

    def store(q, half, tiles):
        for t in range(TILES):
            at = pl.ds(q * PW + half * MW + t * 128, 128)
            out_ref[:, at] = (resid[:, at].astype(F32) + tiles[t]).astype(BF16)

    build(0)
    multiply(0, 0)
    multiply(0, 1)
    first_sends(0)
    multiply(1, 0)
    multiply(1, 1)
    second_sends(0)
    first_sends(1)
    build(1)
    multiply(2, 0)
    multiply(2, 1)
    finish(0)
    second_sends(1)
    first_sends(2)
    multiply(3, 0)
    multiply(3, 1)
    finish(1)
    second_sends(2)
    first_sends(3)
    second_sends(3)
    res_copy.wait()
    finish(2)
    finish(3)

    for copy in core_copies:
        copy.wait_send()
    for number in sorted(messages):
        messages[number].wait_send()


def per_device(packed, block_index, block_sign, ovov, residual_in):
    share, depth, width = packed.shape[0], ovov.shape[0], ovov.shape[1]
    plane = NZ * NX
    count = 4 * 6 + 4
    n_sends = 64
    anywhere = pl.BlockSpec(memory_space=pl.ANY)
    return pl.pallas_call(
        kernel,
        out_shape=jax.ShapeDtypeStruct(residual_in.shape, BF16),
        in_specs=[anywhere] * 5,
        out_specs=pl.BlockSpec(memory_space=pltpu.VMEM),
        scratch_shapes=[
            pltpu.SMEM(block_index.shape, I32),
            pltpu.SMEM(block_sign.shape, I32),
            pltpu.VMEM((plane * HALVES, BLOCK // 2, BLOCK), BF16),
            pltpu.VMEM((depth, width), BF16),
            pltpu.VMEM(residual_in.shape, BF16),
            pltpu.VMEM((4 * BLOCK, depth), BF16),
            pltpu.VMEM((4, 2, 4 * SHARE, PW), F32),
            pltpu.VMEM((4, 4 * SHARE, PW), F32),
            pltpu.VMEM((count, MROWS, 128), I16),
            pltpu.VMEM((count, MROWS, 128), I16),
            pltpu.SemaphoreType.DMA((5,)),
            pltpu.SemaphoreType.DMA((n_sends,)),
            pltpu.SemaphoreType.DMA((NZ * 8,)),
            pltpu.SemaphoreType.DMA((8,)),
            pltpu.SemaphoreType.DMA((8,)),
            pltpu.SemaphoreType.DMA((count,)),
            pltpu.SemaphoreType.DMA((count,)),
        ],
        compiler_params=pltpu.CompilerParams(
            collective_id=0, has_side_effects=True, vmem_limit_bytes=63 << 20
        ),
        cost_estimate=pl.CostEstimate(
            flops=2 * 1024 * depth * width, bytes_accessed=depth * width * 2, transcendentals=0
        ),
    )(
        block_index,
        block_sign,
        packed.reshape(share * 2, BLOCK // 2, BLOCK),
        ovov,
        residual_in,
    )


def solution(mesh):
    in_specs = (
        P(("row", "col", "depth"), None, None),
        P(),
        P(),
        P("row", ("col", "depth")),
        P("row", ("col", "depth")),
    )
    out_specs = P("row", ("col", "depth"))
    return jax.shard_map(
        per_device, mesh=mesh, in_specs=in_specs, out_specs=out_specs, check_vma=False
    )
```

```python
import math

import jax
import jax.numpy as jnp
from jax import lax
from jax.experimental import pallas as pl
from jax.experimental.pallas import tpu as pltpu
from jax.sharding import PartitionSpec as P

MESH = pl.DeviceIdType.MESH
F32 = jnp.float32
BF16 = jnp.bfloat16
I16 = jnp.int16
I32 = jnp.int32

NY, NX, NZ = 4, 4, 4
BLOCK = 128
HALVES = 8
SHARE = 64
STEPS = 64.0
TOP = 32000.0
LN2 = math.log(2.0)

GATHER_ORDER = (
    "e00", "z00", "z01", "x00", "x01", "z10", "n00", "z11", "x10", "x11", "e10", "z20",
    "z21", "x20", "x21", "n10", "e20", "z30", "z31", "x30", "n20", "x31", "n30", "f00",
    "f10", "f20", "f30",
)

UNITS = [(0, 0, 512), (0, 512, 512), (0, 1024, 512), (0, 1536, 512), (1, 0, 512), (1, 512, 512), (1, 1024, 512), (1, 1536, 512)]
ORDER = (
    "b0", "t0", "m0", "d1", "f0", "g0", "d2", "f1", "g1", "d3", "s0", "f2",
    "g2", "s1", "b1", "d4", "f3", "g3", "n0", "s2", "d5", "f4", "g4", "n1",
    "s3", "d6", "f5", "g5", "n2", "s4", "d7", "f6", "g6", "n3", "s5", "f7",
    "g7", "s6", "n4", "s7", "n5", "n6", "n7",
)


def places():
    table, row = {}, 0
    for u, (h, start, width) in enumerate(UNITS):
        for k in range(7 if h == 0 else 6):
            tiles = width // (128 if k == 6 else 256)
            table[u * 7 + k] = (row, tiles)
            row += SHARE * tiles + 16
    return table, row


PLACES, MESSAGE_ROWS = places()


def encode(tiles):
    split = [t.reshape(SHARE // 16, 16, 128) for t in tiles]
    top = jnp.max(jnp.abs(split[0]), axis=0)
    for t in split[1:]:
        top = jnp.maximum(top, jnp.max(jnp.abs(t), axis=0))
    code = jnp.ceil(jnp.log(jnp.maximum(top, 1e-30)) * (STEPS / LN2)) + 1.0
    inverse = jnp.exp(code * (-LN2 / STEPS)) * TOP
    values = [
        jnp.round(t * inverse[None]).astype(I32).astype(I16).reshape(SHARE, 128) for t in split
    ]
    return values, code.astype(I32).astype(I16)


def decode(ref, first, tiles, wanted):
    code = ref[pl.ds(first + SHARE * tiles, 16), :].astype(I32).astype(F32)
    scale = jnp.exp(code * (LN2 / STEPS)) * (1.0 / TOP)
    out = []
    for t in wanted:
        v = ref[pl.ds(first + t * SHARE, SHARE), :].astype(I32).astype(F32)
        out.append((v.reshape(SHARE // 16, 16, 128) * scale[None]).reshape(SHARE, 128))
    return out


def add(a, b):
    return [x + y for x, y in zip(a, b)]


def kernel(
    index_hbm, sign_hbm, packed_ref, ovov_ref, residual_ref, out_ref,
    index_ref, sign_ref, gath, ovov, resid, slab, acc, d2d, msend, mrecv,
    local_sem, gs, gr, ds, dr, ms, mr, entered,
):
    row = lax.axis_index("row")
    col = lax.axis_index("col")
    dep = lax.axis_index("depth")
    core = lax.rem(row, 2)
    y = lax.rem(row // 2, NY)
    zh = row // (2 * NY)

    def row_of(zh_, y_, core_):
        return (zh_ * NY + y_) * 2 + core_

    sibling = {"row": row_of(zh, y, 1 - core)}
    y_up = {"row": row_of(zh, lax.rem(y + 1, NY), core)}
    y_down = {"row": row_of(zh, lax.rem(y + NY - 1, NY), core)}
    z_far = {"row": row_of(1 - zh, y, core)}
    dep_up, dep_down = lax.rem(dep + 1, NX), lax.rem(dep + NX - 1, NX)
    dep_far = lax.rem(dep + 2, NX)
    x_up, x_down = {"depth": dep_up}, {"depth": dep_down}
    z_up, z_down = {"col": lax.rem(col + 1, NZ)}, {"col": lax.rem(col + NZ - 1, NZ)}
    ring_up = {"row": row_of(lax.rem(zh + (col + 1) // NZ, 2), y, core), **z_up}
    ring_down = {
        "row": row_of(lax.rem(zh + 1 + (col + NZ - 1) // NZ, 2), y, core), **z_down
    }

    def slot(c, d):
        return (c * NX + d) * HALVES

    mine = slot(col, dep)
    own_copy = pltpu.make_async_copy(packed_ref, gath.at[pl.ds(mine, HALVES)], local_sem.at[0])
    own_copy.start()
    index_copy = pltpu.make_async_copy(index_hbm, index_ref, local_sem.at[3])
    sign_copy = pltpu.make_async_copy(sign_hbm, sign_ref, local_sem.at[4])
    index_copy.start()
    sign_copy.start()
    res_copy = pltpu.make_async_copy(residual_ref, resid, local_sem.at[1])
    ovov_copy = pltpu.make_async_copy(ovov_ref, ovov, local_sem.at[2])
    ovov_copy.start()
    res_copy.start()

    barrier = pltpu.get_barrier_semaphore()
    peers = (sibling, y_up, y_down, x_up, x_down, ring_up, ring_down)
    for p in peers:
        pl.semaphore_signal(barrier, inc=1, device_id=p, device_id_type=MESH)
    pl.semaphore_wait(barrier, len(peers))
    own_copy.wait()

    def relay(first):
        if not first:
            pl.semaphore_wait(entered, 1)
        pl.semaphore_signal(entered, inc=1, device_id=ring_down, device_id_type=MESH)


    PIECE = HALVES // 2
    sends = {}
    can_up, can_down = col < NZ - 1, col > 0

    def guarded(cond, fn):
        if cond is None:
            fn()
        else:
            pl.when(cond)(fn)

    def both(a, b):
        return b if a is None else jnp.logical_and(a, b)

    def gather_copy(first, sem, number, target):
        part = gath.at[pl.ds(first, PIECE)]
        return pltpu.make_async_remote_copy(
            part, part, gs.at[number], gr.at[sem], device_id=target, device_id_type=MESH
        )

    def send(key, cond, first, sem, target):
        copy = gather_copy(first, sem, len(sends), target)
        sends[key] = [cond, copy, True]
        guarded(cond, copy.start)

    def sent(key):
        cond, copy, flying = sends[key]
        if flying:
            guarded(cond, copy.wait_send)
        sends[key][2] = False

    def arrive(cond, first, sem):
        guarded(cond, gather_copy(first, sem, 0, sibling).wait_recv)

    def rows_at(k):
        if k == 0:
            return [(0, None, col)]
        return [(-1, col >= k, col - k), (1, col + k < NZ, col + k)]

    def z_piece(k, h):
        for side, cond, j in rows_at(k):
            first, sem = slot(j, dep) + h * PIECE, j * 8 + h
            if k > 0:
                arrive(cond, first, sem)
            if side <= 0:
                send(("z", k, h, side, 1), both(cond, can_up), first, sem, z_up)
            if side >= 0:
                send(("z", k, h, side, -1), both(cond, can_down), first, sem, z_down)

    def x_piece(k, h):
        for side, cond, j in rows_at(k):
            send(("x", k, h, side, 1), cond, slot(j, dep) + h * PIECE, j * 8 + 2 + h, x_up)
            send(
                ("x", k, h, side, -1), cond, slot(j, dep) + (1 - h) * PIECE, j * 8 + 5 - h, x_down
            )

    def x_forward(k):
        for side, cond, j in rows_at(k):
            first = slot(j, dep_down)
            arrive(cond, first, j * 8 + 2)
            send(("n", k, 0, side, 1), cond, first, j * 8 + 6, x_up)
            first = slot(j, dep_up) + PIECE
            arrive(cond, first, j * 8 + 5)
            send(("n", k, 0, side, -1), cond, first, j * 8 + 7, x_down)

    def x_last(k):
        for side, cond, j in rows_at(k):
            arrive(cond, slot(j, dep_down) + PIECE, j * 8 + 3)
            arrive(cond, slot(j, dep_up), j * 8 + 4)
            arrive(cond, slot(j, dep_far), j * 8 + 6)
            arrive(cond, slot(j, dep_far) + PIECE, j * 8 + 7)

    def sent_all(kind, k, h):
        for key in sorted(sends):
            if key[:3] == (kind, k, h):
                sent(key)

    for what in GATHER_ORDER:
        k, h = int(what[1]), int(what[2])
        if what[0] == "z":
            z_piece(k, h)
        elif what[0] == "x":
            x_piece(k, h)
        elif what[0] == "n":
            x_forward(k)
        elif what[0] == "f":
            x_last(k)
        elif what[0] == "w":
            sent_all("z", k, h)
        elif what[0] == "v":
            sent_all("x", k, h)
        elif what[0] == "e":
            relay(k == 0)
    for key in sorted(sends):
        sent(key)
    pl.semaphore_wait(entered, 1)
    ovov_copy.wait()
    index_copy.wait()
    sign_copy.wait()

    def block_row(h, i):
        yy = lax.rem(y + (2, 1, NY - 1, 0)[i], NY)
        return ((1 - zh) if h == 0 else zh) * NY + yy

    blocks_per_row = ovov.shape[0] // BLOCK
    HALF = 4 * SHARE

    def build(h):
        for i in range(4):
            r = block_row(h, i)

            @pl.loop(0, blocks_per_row)
            def _(s):
                at = row * blocks_per_row + s
                p = lax.rem(index_ref[r, at], gath.shape[0] // 2)
                sign = sign_ref[r, at].astype(F32)
                there = pl.ds(pl.multiple_of(s * BLOCK, BLOCK), BLOCK)
                for part, c in ((0, 1 - core), (1, core)):
                    tile = gath[2 * p + c]
                    slab[h, pl.ds(part * HALF + i * SHARE, SHARE), there] = (
                        tile.astype(F32) * sign
                    ).astype(BF16)

    core_copies = {}

    def multiply(u, parts):
        h, start, width = UNITS[u]
        rows = pl.ds(parts[0] * HALF, len(parts) * HALF)
        columns = pl.ds(start, width)
        acc[h, rows, columns] = jnp.dot(
            slab[h, rows, :], ovov[:, columns], preferred_element_type=F32
        )
        if 0 not in parts:
            return
        for w in range(2):
            rows = pl.ds(w * 2 * SHARE, 2 * SHARE)
            copy = pltpu.make_async_remote_copy(
                acc.at[h, rows, columns],
                d2d.at[h, rows, columns],
                ds.at[u * 2 + w],
                dr.at[u * 2 + w],
                device_id=sibling,
                device_id_type=MESH,
            )
            copy.start()
            core_copies[u, w] = copy

    def summed(u, i, half):
        h, start, width = UNITS[u]
        rows = pl.ds(i * SHARE, SHARE)
        out = []
        for t in range(width // 256):
            at = pl.ds(start + half * (width // 2) + t * 128, 128)
            out.append(acc[h, pl.ds(HALF + i * SHARE, SHARE), at] + d2d[h, rows, at])
        return out

    messages = {}

    def message_copy(number, target):
        first, tiles = PLACES[number]
        part = pl.ds(first, SHARE * tiles + 16)
        return pltpu.make_async_remote_copy(
            msend.at[part], mrecv.at[part], ms.at[number], mr.at[number],
            device_id=target, device_id_type=MESH,
        )

    def post(number, tiles, target):
        values, code = encode(tiles)
        first, count = PLACES[number]
        for t in range(count):
            msend[pl.ds(first + t * SHARE, SHARE), :] = values[t]
        msend[pl.ds(first + count * SHARE, 16), :] = code
        copy = message_copy(number, target)
        copy.start()
        messages[number] = copy

    def fetch(number):
        message_copy(number, sibling).wait_recv()
        first, count = PLACES[number]
        return decode(mrecv, first, count, range(count))

    A, B = 0, 1
    def first_sends(u):
        core_copies[u, 0].wait_recv()
        post(u * 7 + 0, summed(u, 0, A), y_up)
        post(u * 7 + 1, summed(u, 0, B), y_down)

    def near_sends(u):
        post(u * 7 + 2, summed(u, 1, B), y_up)
        core_copies[u, 1].wait_recv()
        post(u * 7 + 3, summed(u, 2, A), y_down)

    def second_sends(u):
        post(u * 7 + 4, add(summed(u, 1, A), fetch(u * 7 + 0)), y_up)
        post(u * 7 + 5, add(summed(u, 2, B), fetch(u * 7 + 1)), y_down)

    z_came = set()

    def z_tile(column):
        for u, (h, start, width) in enumerate(UNITS):
            if h == 0 and start <= column < start + width:
                number = u * 7 + 6
                if number not in z_came:
                    message_copy(number, sibling).wait_recv()
                    z_came.add(number)
                first, count = PLACES[number]
                return decode(mrecv, first, count, [(column - start) // 128])[0]

    def finish(u):
        h, start, width = UNITS[u]
        totals = []
        for half, direct, carried in ((A, 3, 4), (B, 2, 5)):
            totals += add(add(summed(u, 3, half), fetch(u * 7 + direct)), fetch(u * 7 + carried))
        if h == 0:
            post(u * 7 + 6, totals, z_far)
            return
        for t, total in enumerate(totals):
            column = start + t * 128
            at = pl.ds(column, 128)
            out_ref[:, at] = (resid[:, at].astype(F32) + (total + z_tile(column))).astype(BF16)

    def dots(u):
        multiply(u, (0, 1))

    def dots_theirs(u):
        multiply(u, (0,))

    def dots_mine(u):
        multiply(u, (1,))

    res_copy.wait()
    does = {
        "b": build, "t": dots_theirs, "m": dots_mine, "d": dots, "f": first_sends, "g": near_sends, "s": second_sends,
        "n": finish,
    }
    for what in ORDER:
        does[what[0]](int(what[1:]))

    for key in sorted(core_copies):
        core_copies[key].wait_send()
    for number in sorted(messages):
        messages[number].wait_send()


def per_device(packed, block_index, block_sign, ovov, residual_in):
    share, depth, width = packed.shape[0], ovov.shape[0], ovov.shape[1]
    plane = NZ * NX
    count = 7 * len(UNITS)
    n_sends = 64
    anywhere = pl.BlockSpec(memory_space=pl.ANY)
    return pl.pallas_call(
        kernel,
        out_shape=jax.ShapeDtypeStruct(residual_in.shape, BF16),
        in_specs=[anywhere] * 5,
        out_specs=pl.BlockSpec(memory_space=pltpu.VMEM),
        scratch_shapes=[
            pltpu.SMEM(block_index.shape, I32),
            pltpu.SMEM(block_sign.shape, I32),
            pltpu.VMEM((plane * HALVES, BLOCK // 2, BLOCK), BF16),
            pltpu.VMEM((depth, width), BF16),
            pltpu.VMEM(residual_in.shape, BF16),
            pltpu.VMEM((2, 4 * BLOCK, depth), BF16),
            pltpu.VMEM((2, 8 * SHARE, width), F32),
            pltpu.VMEM((2, 4 * SHARE, width), F32),
            pltpu.VMEM((MESSAGE_ROWS, 128), I16),
            pltpu.VMEM((MESSAGE_ROWS, 128), I16),
            pltpu.SemaphoreType.DMA((5,)),
            pltpu.SemaphoreType.DMA((n_sends,)),
            pltpu.SemaphoreType.DMA((NZ * 8,)),
            pltpu.SemaphoreType.DMA((2 * len(UNITS),)),
            pltpu.SemaphoreType.DMA((2 * len(UNITS),)),
            pltpu.SemaphoreType.DMA((count,)),
            pltpu.SemaphoreType.DMA((count,)),
            pltpu.SemaphoreType.REGULAR,
        ],
        compiler_params=pltpu.CompilerParams(
            collective_id=0, has_side_effects=True, vmem_limit_bytes=63 << 20
        ),
        cost_estimate=pl.CostEstimate(
            flops=2 * 1024 * depth * width, bytes_accessed=depth * width * 2, transcendentals=0
        ),
    )(
        block_index,
        block_sign,
        packed.reshape(share * 2, BLOCK // 2, BLOCK),
        ovov,
        residual_in,
    )


def solution(mesh):
    in_specs = (
        P(("row", "col", "depth"), None, None),
        P(),
        P(),
        P("row", ("col", "depth")),
        P("row", ("col", "depth")),
    )
    out_specs = P("row", ("col", "depth"))
    return jax.shard_map(
        per_device, mesh=mesh, in_specs=in_specs, out_specs=out_specs, check_vma=False
    )
```

```python
import math

import jax
import jax.numpy as jnp
from jax import lax
from jax.experimental import pallas as pl
from jax.experimental.pallas import tpu as pltpu
from jax.sharding import PartitionSpec as P

MESH = pl.DeviceIdType.MESH
F32 = jnp.float32
BF16 = jnp.bfloat16
I16 = jnp.int16
I32 = jnp.int32

NY, NX, NZ = 4, 4, 4
BLOCK = 128
HALVES = 8
SHARE = 64
STEPS = 64.0
TOP = 32000.0
LN2 = math.log(2.0)

GATHER_ORDER = (
    "e00", "z00", "z01", "x00", "x01", "z10", "n00", "z11", "x10", "x11", "e10", "z20",
    "z21", "x20", "x21", "n10", "e20", "z30", "z31", "x30", "n20", "x31", "n30", "f00",
    "f10", "f20", "f30",
)

UNITS = [(0, 0, 512), (0, 512, 512), (0, 1024, 512), (0, 1536, 512), (1, 0, 512), (1, 512, 512), (1, 1024, 512), (1, 1536, 512)]
ORDER = (
    "b0", "t0", "m0", "d1", "f0", "g0", "d2", "f1", "g1", "d3", "f2", "g2",
    "s0", "b1", "d4", "f3", "g3", "s1", "d5", "n0", "s2", "f4", "g4", "d6",
    "n1", "s3", "f5", "g5", "d7", "n2", "s4", "f6", "g6", "n3", "s5", "f7",
    "g7", "s6", "n4", "s7", "n5", "n6", "n7",
)


def places():
    table, row = {}, 0
    for u, (h, start, width) in enumerate(UNITS):
        for k in range(7 if h == 0 else 6):
            tiles = width // (128 if k == 6 else 256)
            table[u * 7 + k] = (row, tiles)
            row += SHARE * tiles + 16
    return table, row


PLACES, MESSAGE_ROWS = places()


def encode(tiles):
    split = [t.reshape(SHARE // 16, 16, 128) for t in tiles]
    top = jnp.max(jnp.abs(split[0]), axis=0)
    for t in split[1:]:
        top = jnp.maximum(top, jnp.max(jnp.abs(t), axis=0))
    code = jnp.ceil(jnp.log(jnp.maximum(top, 1e-30)) * (STEPS / LN2)) + 1.0
    inverse = jnp.exp(code * (-LN2 / STEPS)) * TOP
    values = [
        jnp.round(t * inverse[None]).astype(I32).astype(I16).reshape(SHARE, 128) for t in split
    ]
    return values, code.astype(I32).astype(I16)


def decode(ref, first, tiles, wanted):
    code = ref[pl.ds(first + SHARE * tiles, 16), :].astype(I32).astype(F32)
    scale = jnp.exp(code * (LN2 / STEPS)) * (1.0 / TOP)
    out = []
    for t in wanted:
        v = ref[pl.ds(first + t * SHARE, SHARE), :].astype(I32).astype(F32)
        out.append((v.reshape(SHARE // 16, 16, 128) * scale[None]).reshape(SHARE, 128))
    return out


def add(a, b):
    return [x + y for x, y in zip(a, b)]


def kernel(
    index_hbm, sign_hbm, packed_ref, ovov_ref, residual_ref, out_ref,
    index_ref, sign_ref, gath, ovov, resid, slab, acc, d2d, msend, mrecv,
    local_sem, gs, gr, ds, dr, ms, mr, entered,
):
    row = lax.axis_index("row")
    col = lax.axis_index("col")
    dep = lax.axis_index("depth")
    core = lax.rem(row, 2)
    y = lax.rem(row // 2, NY)
    zh = row // (2 * NY)

    def row_of(zh_, y_, core_):
        return (zh_ * NY + y_) * 2 + core_

    sibling = {"row": row_of(zh, y, 1 - core)}
    y_up = {"row": row_of(zh, lax.rem(y + 1, NY), core)}
    y_down = {"row": row_of(zh, lax.rem(y + NY - 1, NY), core)}
    z_far = {"row": row_of(1 - zh, y, core)}
    dep_up, dep_down = lax.rem(dep + 1, NX), lax.rem(dep + NX - 1, NX)
    dep_far = lax.rem(dep + 2, NX)
    x_up, x_down = {"depth": dep_up}, {"depth": dep_down}
    z_up, z_down = {"col": lax.rem(col + 1, NZ)}, {"col": lax.rem(col + NZ - 1, NZ)}
    ring_up = {"row": row_of(lax.rem(zh + (col + 1) // NZ, 2), y, core), **z_up}
    ring_down = {
        "row": row_of(lax.rem(zh + 1 + (col + NZ - 1) // NZ, 2), y, core), **z_down
    }

    def slot(c, d):
        return (c * NX + d) * HALVES

    mine = slot(col, dep)
    own_copy = pltpu.make_async_copy(packed_ref, gath.at[pl.ds(mine, HALVES)], local_sem.at[0])
    own_copy.start()
    index_copy = pltpu.make_async_copy(index_hbm, index_ref, local_sem.at[3])
    sign_copy = pltpu.make_async_copy(sign_hbm, sign_ref, local_sem.at[4])
    index_copy.start()
    sign_copy.start()
    res_copy = pltpu.make_async_copy(residual_ref, resid, local_sem.at[1])
    ovov_copy = pltpu.make_async_copy(ovov_ref, ovov, local_sem.at[2])
    ovov_copy.start()
    res_copy.start()

    barrier = pltpu.get_barrier_semaphore()
    peers = (sibling, y_up, y_down, x_up, x_down, ring_up, ring_down)
    for p in peers:
        pl.semaphore_signal(barrier, inc=1, device_id=p, device_id_type=MESH)
    pl.semaphore_wait(barrier, len(peers))
    own_copy.wait()

    def relay(first):
        if not first:
            pl.semaphore_wait(entered, 1)
        pl.semaphore_signal(entered, inc=1, device_id=ring_down, device_id_type=MESH)


    PIECE = HALVES // 2
    sends = {}
    can_up, can_down = col < NZ - 1, col > 0

    def guarded(cond, fn):
        if cond is None:
            fn()
        else:
            pl.when(cond)(fn)

    def both(a, b):
        return b if a is None else jnp.logical_and(a, b)

    def gather_copy(first, sem, number, target):
        part = gath.at[pl.ds(first, PIECE)]
        return pltpu.make_async_remote_copy(
            part, part, gs.at[number], gr.at[sem], device_id=target, device_id_type=MESH
        )

    def send(key, cond, first, sem, target):
        copy = gather_copy(first, sem, len(sends), target)
        sends[key] = [cond, copy, True]
        guarded(cond, copy.start)

    def sent(key):
        cond, copy, flying = sends[key]
        if flying:
            guarded(cond, copy.wait_send)
        sends[key][2] = False

    def arrive(cond, first, sem):
        guarded(cond, gather_copy(first, sem, 0, sibling).wait_recv)

    def rows_at(k):
        if k == 0:
            return [(0, None, col)]
        return [(-1, col >= k, col - k), (1, col + k < NZ, col + k)]

    def z_piece(k, h):
        for side, cond, j in rows_at(k):
            first, sem = slot(j, dep) + h * PIECE, j * 8 + h
            if k > 0:
                arrive(cond, first, sem)
            if side <= 0:
                send(("z", k, h, side, 1), both(cond, can_up), first, sem, z_up)
            if side >= 0:
                send(("z", k, h, side, -1), both(cond, can_down), first, sem, z_down)

    def x_piece(k, h):
        for side, cond, j in rows_at(k):
            send(("x", k, h, side, 1), cond, slot(j, dep) + h * PIECE, j * 8 + 2 + h, x_up)
            send(
                ("x", k, h, side, -1), cond, slot(j, dep) + (1 - h) * PIECE, j * 8 + 5 - h, x_down
            )

    def x_forward(k):
        for side, cond, j in rows_at(k):
            first = slot(j, dep_down)
            arrive(cond, first, j * 8 + 2)
            send(("n", k, 0, side, 1), cond, first, j * 8 + 6, x_up)
            first = slot(j, dep_up) + PIECE
            arrive(cond, first, j * 8 + 5)
            send(("n", k, 0, side, -1), cond, first, j * 8 + 7, x_down)

    def x_last(k):
        for side, cond, j in rows_at(k):
            arrive(cond, slot(j, dep_down) + PIECE, j * 8 + 3)
            arrive(cond, slot(j, dep_up), j * 8 + 4)
            arrive(cond, slot(j, dep_far), j * 8 + 6)
            arrive(cond, slot(j, dep_far) + PIECE, j * 8 + 7)

    def sent_all(kind, k, h):
        for key in sorted(sends):
            if key[:3] == (kind, k, h):
                sent(key)

    for what in GATHER_ORDER:
        k, h = int(what[1]), int(what[2])
        if what[0] == "z":
            z_piece(k, h)
        elif what[0] == "x":
            x_piece(k, h)
        elif what[0] == "n":
            x_forward(k)
        elif what[0] == "f":
            x_last(k)
        elif what[0] == "w":
            sent_all("z", k, h)
        elif what[0] == "v":
            sent_all("x", k, h)
        elif what[0] == "e":
            relay(k == 0)
    for key in sorted(sends):
        sent(key)
    pl.semaphore_wait(entered, 1)
    ovov_copy.wait()
    index_copy.wait()
    sign_copy.wait()

    def block_row(h, i):
        yy = lax.rem(y + (2, 1, NY - 1, 0)[i], NY)
        return ((1 - zh) if h == 0 else zh) * NY + yy

    blocks_per_row = ovov.shape[0] // BLOCK
    HALF = 4 * SHARE

    def build(h):
        for i in range(4):
            r = block_row(h, i)

            @pl.loop(0, blocks_per_row)
            def _(s):
                at = row * blocks_per_row + s
                p = lax.rem(index_ref[r, at], gath.shape[0] // 2)
                sign = sign_ref[r, at].astype(F32)
                there = pl.ds(pl.multiple_of(s * BLOCK, BLOCK), BLOCK)
                for part, c in ((0, 1 - core), (1, core)):
                    tile = gath[2 * p + c]
                    slab[h, pl.ds(part * HALF + i * SHARE, SHARE), there] = (
                        tile.astype(F32) * sign
                    ).astype(BF16)

    core_copies = {}

    def multiply(u, parts):
        h, start, width = UNITS[u]
        rows = pl.ds(parts[0] * HALF, len(parts) * HALF)
        columns = pl.ds(start, width)
        acc[h, rows, columns] = jnp.dot(
            slab[h, rows, :], ovov[:, columns], preferred_element_type=F32
        )
        if 0 not in parts:
            return
        for w in range(2):
            rows = pl.ds(w * 2 * SHARE, 2 * SHARE)
            copy = pltpu.make_async_remote_copy(
                acc.at[h, rows, columns],
                d2d.at[h, rows, columns],
                ds.at[u * 2 + w],
                dr.at[u * 2 + w],
                device_id=sibling,
                device_id_type=MESH,
            )
            copy.start()
            core_copies[u, w] = copy

    def summed(u, i, half):
        h, start, width = UNITS[u]
        rows = pl.ds(i * SHARE, SHARE)
        out = []
        for t in range(width // 256):
            at = pl.ds(start + half * (width // 2) + t * 128, 128)
            out.append(acc[h, pl.ds(HALF + i * SHARE, SHARE), at] + d2d[h, rows, at])
        return out

    messages = {}

    def message_copy(number, target):
        first, tiles = PLACES[number]
        part = pl.ds(first, SHARE * tiles + 16)
        return pltpu.make_async_remote_copy(
            msend.at[part], mrecv.at[part], ms.at[number], mr.at[number],
            device_id=target, device_id_type=MESH,
        )

    def post(number, tiles, target):
        values, code = encode(tiles)
        first, count = PLACES[number]
        for t in range(count):
            msend[pl.ds(first + t * SHARE, SHARE), :] = values[t]
        msend[pl.ds(first + count * SHARE, 16), :] = code
        copy = message_copy(number, target)
        copy.start()
        messages[number] = copy

    def fetch(number):
        message_copy(number, sibling).wait_recv()
        first, count = PLACES[number]
        return decode(mrecv, first, count, range(count))

    A, B = 0, 1
    def first_sends(u):
        core_copies[u, 0].wait_recv()
        post(u * 7 + 0, summed(u, 0, A), y_up)
        post(u * 7 + 1, summed(u, 0, B), y_down)

    def near_sends(u):
        post(u * 7 + 2, summed(u, 1, B), y_up)
        core_copies[u, 1].wait_recv()
        post(u * 7 + 3, summed(u, 2, A), y_down)

    def second_sends(u):
        post(u * 7 + 4, add(summed(u, 1, A), fetch(u * 7 + 0)), y_up)
        post(u * 7 + 5, add(summed(u, 2, B), fetch(u * 7 + 1)), y_down)

    z_came = set()

    def z_tile(column):
        for u, (h, start, width) in enumerate(UNITS):
            if h == 0 and start <= column < start + width:
                number = u * 7 + 6
                if number not in z_came:
                    message_copy(number, sibling).wait_recv()
                    z_came.add(number)
                first, count = PLACES[number]
                return decode(mrecv, first, count, [(column - start) // 128])[0]

    def finish(u):
        h, start, width = UNITS[u]
        totals = []
        for half, direct, carried in ((A, 3, 4), (B, 2, 5)):
            totals += add(add(summed(u, 3, half), fetch(u * 7 + direct)), fetch(u * 7 + carried))
        if h == 0:
            post(u * 7 + 6, totals, z_far)
            return
        for t, total in enumerate(totals):
            column = start + t * 128
            at = pl.ds(column, 128)
            out_ref[:, at] = (resid[:, at].astype(F32) + (total + z_tile(column))).astype(BF16)

    def dots(u):
        multiply(u, (0, 1))

    def dots_theirs(u):
        multiply(u, (0,))

    def dots_mine(u):
        multiply(u, (1,))

    res_copy.wait()
    does = {
        "b": build, "t": dots_theirs, "m": dots_mine, "d": dots, "f": first_sends, "g": near_sends, "s": second_sends,
        "n": finish,
    }
    for what in ORDER:
        does[what[0]](int(what[1:]))

    for key in sorted(core_copies):
        core_copies[key].wait_send()
    for number in sorted(messages):
        messages[number].wait_send()


def per_device(packed, block_index, block_sign, ovov, residual_in):
    share, depth, width = packed.shape[0], ovov.shape[0], ovov.shape[1]
    plane = NZ * NX
    count = 7 * len(UNITS)
    n_sends = 64
    anywhere = pl.BlockSpec(memory_space=pl.ANY)
    return pl.pallas_call(
        kernel,
        out_shape=jax.ShapeDtypeStruct(residual_in.shape, BF16),
        in_specs=[anywhere] * 5,
        out_specs=pl.BlockSpec(memory_space=pltpu.VMEM),
        scratch_shapes=[
            pltpu.SMEM(block_index.shape, I32),
            pltpu.SMEM(block_sign.shape, I32),
            pltpu.VMEM((plane * HALVES, BLOCK // 2, BLOCK), BF16),
            pltpu.VMEM((depth, width), BF16),
            pltpu.VMEM(residual_in.shape, BF16),
            pltpu.VMEM((2, 4 * BLOCK, depth), BF16),
            pltpu.VMEM((2, 8 * SHARE, width), F32),
            pltpu.VMEM((2, 4 * SHARE, width), F32),
            pltpu.VMEM((MESSAGE_ROWS, 128), I16),
            pltpu.VMEM((MESSAGE_ROWS, 128), I16),
            pltpu.SemaphoreType.DMA((5,)),
            pltpu.SemaphoreType.DMA((n_sends,)),
            pltpu.SemaphoreType.DMA((NZ * 8,)),
            pltpu.SemaphoreType.DMA((2 * len(UNITS),)),
            pltpu.SemaphoreType.DMA((2 * len(UNITS),)),
            pltpu.SemaphoreType.DMA((count,)),
            pltpu.SemaphoreType.DMA((count,)),
            pltpu.SemaphoreType.REGULAR,
        ],
        compiler_params=pltpu.CompilerParams(
            collective_id=0, has_side_effects=True, vmem_limit_bytes=63 << 20
        ),
        cost_estimate=pl.CostEstimate(
            flops=2 * 1024 * depth * width, bytes_accessed=depth * width * 2, transcendentals=0
        ),
    )(
        block_index,
        block_sign,
        packed.reshape(share * 2, BLOCK // 2, BLOCK),
        ovov,
        residual_in,
    )


def solution(mesh):
    in_specs = (
        P(("row", "col", "depth"), None, None),
        P(),
        P(),
        P("row", ("col", "depth")),
        P("row", ("col", "depth")),
    )
    out_specs = P("row", ("col", "depth"))
    return jax.shard_map(
        per_device, mesh=mesh, in_specs=in_specs, out_specs=out_specs, check_vma=False
    )
```

```python
import math

import jax
import jax.numpy as jnp
from jax import lax
from jax.experimental import pallas as pl
from jax.experimental.pallas import tpu as pltpu
from jax.sharding import PartitionSpec as P

MESH = pl.DeviceIdType.MESH
F32 = jnp.float32
BF16 = jnp.bfloat16
I16 = jnp.int16
I32 = jnp.int32

NY, NX, NZ = 4, 4, 4
BLOCK = 128
HALVES = 8
SHARE = 64
STEPS = 64.0
TOP = 32000.0
LN2 = math.log(2.0)

GATHER_ORDER = (
    "e00", "z00", "z01", "x00", "x01", "z10", "n00", "z11", "x10", "x11", "e10", "z20",
    "z21", "x20", "x21", "n10", "e20", "z30", "z31", "x30", "n20", "x31", "n30", "f00",
    "f10", "f20", "f30",
)

UNITS = [(0, 0, 512), (0, 512, 512), (0, 1024, 512), (0, 1536, 512), (1, 0, 512), (1, 512, 512), (1, 1024, 512), (1, 1536, 512)]
ORDER = (
    "b0", "t0", "m0", "d1", "f0", "g0", "d2", "f1", "g1", "d3", "f2", "g2",
    "s0", "b1", "d4", "f3", "g3", "s1", "d5", "n0", "s2", "f4", "g4", "d6",
    "n1", "s3", "f5", "g5", "d7", "n2", "s4", "f6", "g6", "n3", "s5", "f7",
    "g7", "s6", "n4", "s7", "n5", "n6", "n7",
)


def places():
    table, row = {}, 0
    for u, (h, start, width) in enumerate(UNITS):
        for k in range(7 if h == 0 else 6):
            tiles = width // (128 if k == 6 else 256)
            table[u * 7 + k] = (row, tiles)
            row += SHARE * tiles + 16
    return table, row


PLACES, MESSAGE_ROWS = places()


def encode(tiles):
    split = [t.reshape(SHARE // 16, 16, 128) for t in tiles]
    top = jnp.max(jnp.abs(split[0]), axis=0)
    for t in split[1:]:
        top = jnp.maximum(top, jnp.max(jnp.abs(t), axis=0))
    code = jnp.ceil(jnp.log(jnp.maximum(top, 1e-30)) * (STEPS / LN2)) + 1.0
    inverse = jnp.exp(code * (-LN2 / STEPS)) * TOP
    values = [
        jnp.round(t * inverse[None]).astype(I32).astype(I16).reshape(SHARE, 128) for t in split
    ]
    return values, code.astype(I32).astype(I16)


def decode(ref, first, tiles, wanted):
    code = ref[pl.ds(first + SHARE * tiles, 16), :].astype(I32).astype(F32)
    scale = jnp.exp(code * (LN2 / STEPS)) * (1.0 / TOP)
    out = []
    for t in wanted:
        v = ref[pl.ds(first + t * SHARE, SHARE), :].astype(I32).astype(F32)
        out.append((v.reshape(SHARE // 16, 16, 128) * scale[None]).reshape(SHARE, 128))
    return out


def add(a, b):
    return [x + y for x, y in zip(a, b)]


def kernel(
    index_hbm, sign_hbm, packed_ref, ovov_ref, residual_ref, out_ref,
    index_ref, sign_ref, gath, ovov, resid, slab, acc, d2d, msend, mrecv,
    local_sem, gs, gr, ds, dr, ms, mr, entered,
):
    row = lax.axis_index("row")
    col = lax.axis_index("col")
    dep = lax.axis_index("depth")
    core = lax.rem(row, 2)
    y = lax.rem(row // 2, NY)
    zh = row // (2 * NY)

    def row_of(zh_, y_, core_):
        return (zh_ * NY + y_) * 2 + core_

    sibling = {"row": row_of(zh, y, 1 - core)}
    y_up = {"row": row_of(zh, lax.rem(y + 1, NY), core)}
    y_down = {"row": row_of(zh, lax.rem(y + NY - 1, NY), core)}
    z_far = {"row": row_of(1 - zh, y, core)}
    dep_up, dep_down = lax.rem(dep + 1, NX), lax.rem(dep + NX - 1, NX)
    dep_far = lax.rem(dep + 2, NX)
    x_up, x_down = {"depth": dep_up}, {"depth": dep_down}
    z_up, z_down = {"col": lax.rem(col + 1, NZ)}, {"col": lax.rem(col + NZ - 1, NZ)}
    ring_up = {"row": row_of(lax.rem(zh + (col + 1) // NZ, 2), y, core), **z_up}
    ring_down = {
        "row": row_of(lax.rem(zh + 1 + (col + NZ - 1) // NZ, 2), y, core), **z_down
    }

    def slot(c, d):
        return (c * NX + d) * HALVES

    mine = slot(col, dep)
    own_copy = pltpu.make_async_copy(packed_ref, gath.at[pl.ds(mine, HALVES)], local_sem.at[0])
    own_copy.start()
    index_copy = pltpu.make_async_copy(index_hbm, index_ref, local_sem.at[3])
    sign_copy = pltpu.make_async_copy(sign_hbm, sign_ref, local_sem.at[4])
    index_copy.start()
    sign_copy.start()
    res_copy = pltpu.make_async_copy(residual_ref, resid, local_sem.at[1])
    ovov_copy = pltpu.make_async_copy(ovov_ref, ovov, local_sem.at[2])
    ovov_copy.start()
    res_copy.start()

    barrier = pltpu.get_barrier_semaphore()
    peers = (sibling, y_up, y_down, x_up, x_down, ring_up, ring_down)
    for p in peers:
        pl.semaphore_signal(barrier, inc=1, device_id=p, device_id_type=MESH)
    pl.semaphore_wait(barrier, len(peers))
    own_copy.wait()

    def relay(first):
        if not first:
            pl.semaphore_wait(entered, 1)
        pl.semaphore_signal(entered, inc=1, device_id=ring_down, device_id_type=MESH)


    PIECE = HALVES // 2
    sends = {}
    can_up, can_down = col < NZ - 1, col > 0

    def guarded(cond, fn):
        if cond is None:
            fn()
        else:
            pl.when(cond)(fn)

    def both(a, b):
        return b if a is None else jnp.logical_and(a, b)

    def gather_copy(first, sem, number, target):
        part = gath.at[pl.ds(first, PIECE)]
        return pltpu.make_async_remote_copy(
            part, part, gs.at[number], gr.at[sem], device_id=target, device_id_type=MESH
        )

    def send(key, cond, first, sem, target):
        copy = gather_copy(first, sem, len(sends), target)
        sends[key] = [cond, copy, True]
        guarded(cond, copy.start)

    def sent(key):
        cond, copy, flying = sends[key]
        if flying:
            guarded(cond, copy.wait_send)
        sends[key][2] = False

    def arrive(cond, first, sem):
        guarded(cond, gather_copy(first, sem, 0, sibling).wait_recv)

    def rows_at(k):
        if k == 0:
            return [(0, None, col)]
        return [(-1, col >= k, col - k), (1, col + k < NZ, col + k)]

    def z_piece(k, h):
        for side, cond, j in rows_at(k):
            first, sem = slot(j, dep) + h * PIECE, j * 8 + h
            if k > 0:
                arrive(cond, first, sem)
            if side <= 0:
                send(("z", k, h, side, 1), both(cond, can_up), first, sem, z_up)
            if side >= 0:
                send(("z", k, h, side, -1), both(cond, can_down), first, sem, z_down)

    def x_piece(k, h):
        for side, cond, j in rows_at(k):
            send(("x", k, h, side, 1), cond, slot(j, dep) + h * PIECE, j * 8 + 2 + h, x_up)
            send(
                ("x", k, h, side, -1), cond, slot(j, dep) + (1 - h) * PIECE, j * 8 + 5 - h, x_down
            )

    def x_forward(k):
        for side, cond, j in rows_at(k):
            first = slot(j, dep_down)
            arrive(cond, first, j * 8 + 2)
            send(("n", k, 0, side, 1), cond, first, j * 8 + 6, x_up)
            first = slot(j, dep_up) + PIECE
            arrive(cond, first, j * 8 + 5)
            send(("n", k, 0, side, -1), cond, first, j * 8 + 7, x_down)

    def x_last(k):
        for side, cond, j in rows_at(k):
            arrive(cond, slot(j, dep_down) + PIECE, j * 8 + 3)
            arrive(cond, slot(j, dep_up), j * 8 + 4)
            arrive(cond, slot(j, dep_far), j * 8 + 6)
            arrive(cond, slot(j, dep_far) + PIECE, j * 8 + 7)

    def sent_all(kind, k, h):
        for key in sorted(sends):
            if key[:3] == (kind, k, h):
                sent(key)

    for what in GATHER_ORDER:
        k, h = int(what[1]), int(what[2])
        if what[0] == "z":
            z_piece(k, h)
        elif what[0] == "x":
            x_piece(k, h)
        elif what[0] == "n":
            x_forward(k)
        elif what[0] == "f":
            x_last(k)
        elif what[0] == "w":
            sent_all("z", k, h)
        elif what[0] == "v":
            sent_all("x", k, h)
        elif what[0] == "e":
            relay(k == 0)
    ovov_copy.wait()
    index_copy.wait()
    sign_copy.wait()

    def block_row(h, i):
        yy = lax.rem(y + (2, 1, NY - 1, 0)[i], NY)
        return ((1 - zh) if h == 0 else zh) * NY + yy

    blocks_per_row = ovov.shape[0] // BLOCK
    HALF = 4 * SHARE

    def build(h):
        for i in range(4):
            r = block_row(h, i)

            @pl.loop(0, blocks_per_row)
            def _(s):
                at = row * blocks_per_row + s
                p = lax.rem(index_ref[r, at], gath.shape[0] // 2)
                sign = sign_ref[r, at].astype(F32)
                there = pl.ds(pl.multiple_of(s * BLOCK, BLOCK), BLOCK)
                for part, c in ((0, 1 - core), (1, core)):
                    tile = gath[2 * p + c]
                    slab[h, pl.ds(part * HALF + i * SHARE, SHARE), there] = (
                        tile.astype(F32) * sign
                    ).astype(BF16)

    core_copies = {}

    def multiply(u, parts):
        h, start, width = UNITS[u]
        rows = pl.ds(parts[0] * HALF, len(parts) * HALF)
        columns = pl.ds(start, width)
        acc[h, rows, columns] = jnp.dot(
            slab[h, rows, :], ovov[:, columns], preferred_element_type=F32
        )
        if 0 not in parts:
            return
        for w in range(2):
            rows = pl.ds(w * 2 * SHARE, 2 * SHARE)
            copy = pltpu.make_async_remote_copy(
                acc.at[h, rows, columns],
                d2d.at[h, rows, columns],
                ds.at[u * 2 + w],
                dr.at[u * 2 + w],
                device_id=sibling,
                device_id_type=MESH,
            )
            copy.start()
            core_copies[u, w] = copy

    def summed(u, i, half):
        h, start, width = UNITS[u]
        rows = pl.ds(i * SHARE, SHARE)
        out = []
        for t in range(width // 256):
            at = pl.ds(start + half * (width // 2) + t * 128, 128)
            out.append(acc[h, pl.ds(HALF + i * SHARE, SHARE), at] + d2d[h, rows, at])
        return out

    messages = {}

    def message_copy(number, target):
        first, tiles = PLACES[number]
        part = pl.ds(first, SHARE * tiles + 16)
        return pltpu.make_async_remote_copy(
            msend.at[part], mrecv.at[part], ms.at[number], mr.at[number],
            device_id=target, device_id_type=MESH,
        )

    def post(number, tiles, target):
        values, code = encode(tiles)
        first, count = PLACES[number]
        for t in range(count):
            msend[pl.ds(first + t * SHARE, SHARE), :] = values[t]
        msend[pl.ds(first + count * SHARE, 16), :] = code
        copy = message_copy(number, target)
        copy.start()
        messages[number] = copy

    def fetch(number):
        message_copy(number, sibling).wait_recv()
        first, count = PLACES[number]
        return decode(mrecv, first, count, range(count))

    A, B = 0, 1
    def first_sends(u):
        core_copies[u, 0].wait_recv()
        post(u * 7 + 0, summed(u, 0, A), y_up)
        post(u * 7 + 1, summed(u, 0, B), y_down)

    def near_sends(u):
        post(u * 7 + 2, summed(u, 1, B), y_up)
        core_copies[u, 1].wait_recv()
        post(u * 7 + 3, summed(u, 2, A), y_down)

    def second_sends(u):
        post(u * 7 + 4, add(summed(u, 1, A), fetch(u * 7 + 0)), y_up)
        post(u * 7 + 5, add(summed(u, 2, B), fetch(u * 7 + 1)), y_down)

    z_came = set()

    def z_tile(column):
        for u, (h, start, width) in enumerate(UNITS):
            if h == 0 and start <= column < start + width:
                number = u * 7 + 6
                if number not in z_came:
                    message_copy(number, sibling).wait_recv()
                    z_came.add(number)
                first, count = PLACES[number]
                return decode(mrecv, first, count, [(column - start) // 128])[0]

    def finish(u):
        h, start, width = UNITS[u]
        totals = []
        for half, direct, carried in ((A, 3, 4), (B, 2, 5)):
            totals += add(add(summed(u, 3, half), fetch(u * 7 + direct)), fetch(u * 7 + carried))
        if h == 0:
            post(u * 7 + 6, totals, z_far)
            return
        for t, total in enumerate(totals):
            column = start + t * 128
            at = pl.ds(column, 128)
            out_ref[:, at] = (resid[:, at].astype(F32) + (total + z_tile(column))).astype(BF16)

    def dots(u):
        multiply(u, (0, 1))

    def dots_theirs(u):
        multiply(u, (0,))

    def dots_mine(u):
        multiply(u, (1,))

    res_copy.wait()
    does = {
        "b": build, "t": dots_theirs, "m": dots_mine, "d": dots, "f": first_sends, "g": near_sends, "s": second_sends,
        "n": finish,
    }
    for what in ORDER:
        if what == "n0":
            pl.semaphore_wait(entered, 1)
        does[what[0]](int(what[1:]))

    for key in sorted(sends):
        sent(key)
    for key in sorted(core_copies):
        core_copies[key].wait_send()
    for number in sorted(messages):
        messages[number].wait_send()


def per_device(packed, block_index, block_sign, ovov, residual_in):
    share, depth, width = packed.shape[0], ovov.shape[0], ovov.shape[1]
    plane = NZ * NX
    count = 7 * len(UNITS)
    n_sends = 64
    anywhere = pl.BlockSpec(memory_space=pl.ANY)
    return pl.pallas_call(
        kernel,
        out_shape=jax.ShapeDtypeStruct(residual_in.shape, BF16),
        in_specs=[anywhere] * 5,
        out_specs=pl.BlockSpec(memory_space=pltpu.VMEM),
        scratch_shapes=[
            pltpu.SMEM(block_index.shape, I32),
            pltpu.SMEM(block_sign.shape, I32),
            pltpu.VMEM((plane * HALVES, BLOCK // 2, BLOCK), BF16),
            pltpu.VMEM((depth, width), BF16),
            pltpu.VMEM(residual_in.shape, BF16),
            pltpu.VMEM((2, 4 * BLOCK, depth), BF16),
            pltpu.VMEM((2, 8 * SHARE, width), F32),
            pltpu.VMEM((2, 4 * SHARE, width), F32),
            pltpu.VMEM((MESSAGE_ROWS, 128), I16),
            pltpu.VMEM((MESSAGE_ROWS, 128), I16),
            pltpu.SemaphoreType.DMA((5,)),
            pltpu.SemaphoreType.DMA((n_sends,)),
            pltpu.SemaphoreType.DMA((NZ * 8,)),
            pltpu.SemaphoreType.DMA((2 * len(UNITS),)),
            pltpu.SemaphoreType.DMA((2 * len(UNITS),)),
            pltpu.SemaphoreType.DMA((count,)),
            pltpu.SemaphoreType.DMA((count,)),
            pltpu.SemaphoreType.REGULAR,
        ],
        compiler_params=pltpu.CompilerParams(
            collective_id=0, has_side_effects=True, vmem_limit_bytes=63 << 20
        ),
        cost_estimate=pl.CostEstimate(
            flops=2 * 1024 * depth * width, bytes_accessed=depth * width * 2, transcendentals=0
        ),
    )(
        block_index,
        block_sign,
        packed.reshape(share * 2, BLOCK // 2, BLOCK),
        ovov,
        residual_in,
    )


def solution(mesh):
    in_specs = (
        P(("row", "col", "depth"), None, None),
        P(),
        P(),
        P("row", ("col", "depth")),
        P("row", ("col", "depth")),
    )
    out_specs = P("row", ("col", "depth"))
    return jax.shard_map(
        per_device, mesh=mesh, in_specs=in_specs, out_specs=out_specs, check_vma=False
    )
```
